32 devices in a mesh: tile: 16 (over z, x, core), member: 2 (over y).
Axes of the slice: x: 2, y: 2, z: 4, core: 2. Of those that a mesh axis runs over, the one named last changes fastest.
Arguments:
- tracers: float32 [4, 12, 4, 192, 256], P('member', None, None, 'tile'), may hold values from -4 to 4
- hydro: float32 [15, 192, 256], P(None, 'tile', 'member'), may hold values from -6 to 6, as said below
- wet: int32 [192, 256], P('tile'), may hold values from 0 to 1, as said below
- rates: float32 [4, 12, 12], P('member'), may hold values from -1.75 to 1.75
- decays: float32 [4, 12], P('member'), may hold values from 0.1 to 2
Outputs:
- final: float32 [4, 12, 4, 192, 256], P('member', None, None, 'tile')
The draws below stay inside these ranges and needn't reach their ends.
Inputs may be any that keep to these rules, and one draw needn't show every extreme that they name: The wet mask is 0 or 1. `hydro`: planes 8 to 14 lie within -3 to 3.
All inputs are finite; a program needn't handle non-finite values.
Results may differ from the reference program's by a relative error of at most 0.0001.
Values sent between devices are 32-bit elements; how exact they have to be, the bound alone decides.
A program may use at most 128 MiB of HBM per device.

```python
import math
import jax
import jax.numpy as jnp
from jax import lax

ROWS_DEV = 12
TRACERS = 12
LAYERS = 4
HYDRO = 15
STEPS = 2
NX = 192
NY = 256
MEMBERS = 4


def draw_wet(key, part):
    key = jax.random.fold_in(key, 7)
    row_ids = jnp.arange(NX, dtype=jnp.int32)
    local = row_ids % ROWS_DEV
    near_edge = (local < 2) | (local >= ROWS_DEV - 2)
    spread = 128 + 896 * (row_ids * 37 % NX) // NX
    thresh = jnp.where(near_edge, 960, spread)
    picks = jax.random.randint(key, (NX, NY), 0, 1024, dtype=jnp.int32)
    return (picks < thresh[:, None]).astype(jnp.int32)


def draw_hydro(key, part):
    key = jax.random.fold_in(key, 11)
    key_base, key_strong, key_sign = jax.random.split(key, 3)
    shape = (HYDRO, NX, NY)
    base = jnp.clip(jax.random.normal(key_base, shape, jnp.float32), -3.0, 3.0)
    strong = jax.random.uniform(key_strong, shape, jnp.float32, 4.5, 6.0)
    signs = jnp.where(jax.random.bernoulli(key_sign, 0.5, shape), 1.0, -1.0)
    local = jnp.arange(NX, dtype=jnp.int32) % ROWS_DEV
    near_edge = (local < 2) | (local >= ROWS_DEV - 2)
    planes = jnp.arange(HYDRO, dtype=jnp.int32)
    row_velocity = (planes >= 4) & (planes < 8)
    chosen = row_velocity[:, None, None] & near_edge[None, :, None]
    return jnp.where(chosen, signs * strong, base).astype(jnp.float32)


def draw_tracers(key, part):
    key = jax.random.fold_in(key, 13)
    key_base, key_large, key_sign = jax.random.split(key, 3)
    shape = (MEMBERS, TRACERS, LAYERS, NX, NY)
    base = jnp.clip(0.8 * jax.random.normal(key_base, shape, jnp.float32), -3.5, 3.5)
    large = jax.random.uniform(key_large, shape, jnp.float32, 2.5, 4.0)
    signs = jnp.where(jax.random.bernoulli(key_sign, 0.5, shape), 1.0, -1.0)
    local = jnp.arange(NX, dtype=jnp.int32) % ROWS_DEV
    far_rows = (local == ROWS_DEV - 4) | (local == 3)
    return jnp.where(far_rows[:, None], signs * large, base).astype(jnp.float32)


def levels(rng, extent, cuts, low, top_value):
    loudness = 1.0
    for dim, shards_of in cuts:
        draws = jax.random.uniform(jax.random.fold_in(jax.random.fold_in(rng, 6), dim), (shards_of,), jnp.float32, low / len(cuts), top_value / len(cuts))
        loudness = loudness * jnp.repeat(jnp.exp(draws), extent[dim] // shards_of).reshape((-1,) + (1,) * (len(extent) - 1 - dim))
    return loudness


def centred(stream_key, extent, scale, bound, cuts=(), held_as=jnp.bfloat16):
    level = levels(stream_key, extent, cuts, -0.22, 0.18) if cuts else 1.0
    array = jax.random.normal(stream_key, extent, jnp.float32) * scale * level
    return jnp.minimum(jnp.maximum(array, -bound), bound).astype(held_as)


def setup_inputs(seed: int = 0) -> dict:
    seeds = jax.random.split(jax.random.key(seed), 6)
    return {
        "tracers": draw_tracers(jax.random.fold_in(seeds[5], 71), 0),
        "hydro": draw_hydro(jax.random.fold_in(seeds[5], 71), 0),
        "wet": draw_wet(jax.random.fold_in(seeds[5], 71), 0),
        "rates": centred(seeds[3], (MEMBERS, TRACERS, TRACERS), TRACERS ** -0.5, 1.75, ((0, 2),), jnp.float32),
        "decays": jnp.clip(jnp.exp(math.log(2.0) - 2.9957323 * jax.random.uniform(seeds[4], (MEMBERS, TRACERS), jnp.float32) ** levels(seeds[4], (MEMBERS, TRACERS), ((0, 2),), -0.2, 0.2)), 0.1, 2.0),
    }


def advance(conc, fields, rate, decay):
    inner = conc[..., 2:-2, :]
    padded = jnp.pad(inner, ((0, 0), (0, 0), (0, 0), (0, 0), (2, 2)))
    width = inner.shape[-1]
    east1 = padded[..., 3:width + 3]
    west1 = padded[..., 1:width + 1]
    east2 = padded[..., 4:width + 4]
    west2 = padded[..., 0:width]
    rows = conc.shape[3]
    south1 = conc[..., 3:rows - 1, :]
    north1 = conc[..., 1:rows - 3, :]
    south2 = conc[..., 4:, :]
    north2 = conc[..., :rows - 4, :]
    deriv_x = (8.0 * (east1 - west1) - (east2 - west2)) / 12.0
    deriv_y = (8.0 * (south1 - north1) - (south2 - north2)) / 12.0
    lapl = south1 + north1 + east1 + west1 - 4.0 * inner
    vel_x = 0.5 * fields[0:4]
    vel_y = 0.5 * fields[4:8]
    kappa = 0.1 * jnp.exp(0.7 * fields[8:12])
    mixing = 0.05 * jnp.exp(0.7 * fields[12:15])
    mask = fields[15]
    flux = mixing * (inner[:, :, 1:] - inner[:, :, :-1])
    zero_plane = jnp.zeros_like(flux[:, :, :1])
    vert = jnp.concatenate([flux, zero_plane], axis=2) - jnp.concatenate([zero_plane, flux], axis=2)
    react = jnp.einsum("mst,mtlrc->mslrc", rate, jnp.tanh(inner), precision=lax.Precision.HIGHEST)
    react = react - decay[:, :, None, None, None] * inner
    tend = -vel_x * deriv_x - vel_y * deriv_y + kappa * lapl + vert + react
    return mask * (inner + 0.2 * tend)


def reference(tracers, hydro, wet, rates, decays):
    fields = jnp.concatenate([hydro, wet.astype(jnp.float32)[None]], axis=0)

    def one_member(items):
        conc, rate, decay = items
        conc = conc[None]
        for step in range(STEPS):
            padded = jnp.pad(conc, ((0, 0), (0, 0), (0, 0), (2, 2), (0, 0)))
            conc = advance(padded, fields, rate[None], decay[None])
        return conc[0]

    return lax.map(one_member, (tracers, rates, decays))
```

```python
import functools

import jax
import jax.numpy as jnp
from jax import lax
from jax.experimental import pallas as pl
from jax.experimental.pallas import tpu as pltpu
from jax.sharding import PartitionSpec as P

SUB, LANE = 8, 128
CHUNK = 4


def kernel(
    members, tiles, tr, hyin, wet, rates, decays, out,
    c0, c1, hy, msk, coef, wmain, wlow, dec,
    load_sem, tr_send, tr_recv, hy_send, hy_recv, up_send, up_recv, dn_send, dn_recv,
    wet_send, wet_recv,
):
    local_m, tracers = rates.shape[0], rates.shape[1]
    rows, pairs = tr.shape[1], tr.shape[2]
    wide = tracers * SUB
    tile = lax.axis_index("tile")
    member = lax.axis_index("member")
    has_up = tile > 0
    has_dn = tile < tiles - 1

    barrier = pltpu.get_barrier_semaphore()

    def greet(where):
        pl.semaphore_signal(barrier, inc=1, device_id=where, device_id_type=pl.DeviceIdType.MESH)

    def other(d):
        return lax.rem(member + d, members)

    for d in range(1, members):
        greet({"tile": tile, "member": other(d)})

    @pl.when(has_up)
    def _():
        for d in range(members):
            greet({"tile": tile - 1, "member": other(d)})

    @pl.when(has_dn)
    def _():
        for d in range(members):
            greet({"tile": tile + 1, "member": other(d)})

    load_tr = pltpu.make_async_copy(tr, c0.at[:, pl.ds(4, rows)], load_sem.at[0])
    load_hy = pltpu.make_async_copy(hyin, hy.at[member, pl.ds(2, rows)], load_sem.at[1])
    load_tr.start()
    load_hy.start()

    sub = lax.broadcasted_iota(jnp.int32, (SUB, LANE), 0)
    lane = lax.broadcasted_iota(jnp.int32, (SUB, LANE), 1)
    left = sub < 4
    for r in range(rows):
        for p in range(pairs):
            a = jnp.broadcast_to(wet[r : r + 1, 2 * p * LANE : (2 * p + 1) * LANE], (SUB, LANE))
            b = jnp.broadcast_to(wet[r : r + 1, (2 * p + 1) * LANE : (2 * p + 2) * LANE], (SUB, LANE))
            msk[r + 2, p] = jnp.where(left, a, b).astype(jnp.float32)

    def remote(src, dst, send, recv, where):
        return pltpu.make_async_remote_copy(
            src_ref=src, dst_ref=dst, send_sem=send, recv_sem=recv,
            device_id=where, device_id_type=pl.DeviceIdType.MESH,
        )

    def tr_copy(k):
        source, target = ((0, rows + 4), (rows - 2, 2), (2, rows + 6), (rows - 4, 0))[k]
        step = -1 if k % 2 == 0 else 1
        return remote(
            tr.at[:, pl.ds(source, 2)], c0.at[:, pl.ds(target, 2)], tr_send.at[k], tr_recv.at[k],
            {"tile": tile + step, "member": member},
        )

    def hy_copy(d, slot):
        return remote(
            hyin, hy.at[slot, pl.ds(2, rows)], hy_send.at[d - 1], hy_recv.at[d - 1],
            {"tile": tile, "member": other(d)},
        )

    def up_copy(d, slot):
        return remote(
            hyin.at[pl.ds(0, 2)], hy.at[slot, pl.ds(rows + 2, 2)], up_send.at[d], up_recv.at[d],
            {"tile": tile - 1, "member": other(d)},
        )

    def dn_copy(d, slot):
        return remote(
            hyin.at[pl.ds(rows - 2, 2)], hy.at[slot, pl.ds(0, 2)], dn_send.at[d], dn_recv.at[d],
            {"tile": tile + 1, "member": other(d)},
        )

    def wet_copy(k):
        source, target = ((2, rows + 2), (rows, 0))[k]
        step = -1 if k == 0 else 1
        return remote(
            msk.at[pl.ds(source, 2)], msk.at[pl.ds(target, 2)], wet_send.at[k], wet_recv.at[k],
            {"tile": tile + step, "member": member},
        )

    partners = members - 1 + members * (has_up.astype(jnp.int32) + has_dn.astype(jnp.int32))
    pl.semaphore_wait(barrier, partners)

    for d in range(1, members):
        hy_copy(d, member).start()

    @pl.when(has_up)
    def _():
        tr_copy(0).start()
        for d in range(members):
            up_copy(d, member).start()
        wet_copy(0).start()
        tr_copy(2).start()

    @pl.when(has_dn)
    def _():
        tr_copy(1).start()
        for d in range(members):
            dn_copy(d, member).start()
        wet_copy(1).start()
        tr_copy(3).start()

    @pl.when(jnp.logical_not(has_up))
    def _():
        c0[:, 0:4] = jnp.zeros_like(c0[:, 0:4])
        hy[:, 0:2] = jnp.zeros_like(hy[:, 0:2])
        msk[0:2] = jnp.zeros_like(msk[0:2])

    @pl.when(jnp.logical_not(has_dn))
    def _():
        c0[:, rows + 4 :] = jnp.zeros_like(c0[:, rows + 4 :])
        hy[:, rows + 2 :] = jnp.zeros_like(hy[:, rows + 2 :])
        msk[rows + 2 :] = jnp.zeros_like(msk[rows + 2 :])

    for m in range(local_m):
        spread = jnp.broadcast_to(rates[m][:, None, :], (tracers, SUB, tracers)).reshape(wide, tracers)
        row_t = lax.broadcasted_iota(jnp.int32, (tracers, 2 * wide), 0)
        col_t = lax.broadcasted_iota(jnp.int32, (tracers, 2 * wide), 1)
        pick = (lax.rem(col_t, wide) // SUB == row_t).astype(jnp.float32)
        full = jnp.dot(spread, pick, precision=lax.Precision.HIGHEST, preferred_element_type=jnp.float32)
        row_a = lax.broadcasted_iota(jnp.int32, (wide, 2 * wide), 0)
        col_a = lax.broadcasted_iota(jnp.int32, (wide, 2 * wide), 1)
        full = jnp.where(lax.rem(row_a, SUB) == lax.rem(col_a, SUB), full, 0.0)
        high = full.astype(jnp.bfloat16)
        wmain[m] = high
        wlow[m] = (full - high.astype(jnp.float32)).astype(jnp.bfloat16)[:, :wide]
        row_d = lax.broadcasted_iota(jnp.int32, (wide, tracers), 0)
        col_d = lax.broadcasted_iota(jnp.int32, (wide, tracers), 1)
        loss = jnp.where(row_d // SUB == col_d, jnp.broadcast_to(decays[m : m + 1, :], (wide, tracers)), 0.0)
        loss = jnp.broadcast_to(jnp.sum(loss, axis=1, keepdims=True), (wide, LANE))
        dec[m * tracers : (m + 1) * tracers] = loss.reshape(tracers, SUB, LANE)

    inner_layer = lax.rem(sub, 4) != 3

    def coefficients(start, stride, count):
        def body(k, carry):
            r = start + stride * k + 2
            for p in range(pairs):
                pad = jnp.zeros((1, LANE), jnp.float32)
                a0 = hy[2 * p, r, 0:8]
                b0 = hy[2 * p + 1, r, 0:8]
                a1 = jnp.concatenate([hy[2 * p, r, 8:15], pad], axis=0)
                b1 = jnp.concatenate([hy[2 * p + 1, r, 8:15], pad], axis=0)
                u = 0.5 * jnp.where(left, a0, pltpu.roll(b0, 4, 0))
                v = 0.5 * jnp.where(left, pltpu.roll(a0, 4, 0), b0)
                kappa = 0.1 * jnp.exp(0.7 * jnp.where(left, a1, pltpu.roll(b1, 4, 0)))
                kz = 0.05 * jnp.exp(0.7 * jnp.where(left, pltpu.roll(a1, 4, 0), b1))
                kz = jnp.where(inner_layer, kz, 0.0)
                mask = msk[r, p]
                s = 0.2 * mask
                kk = s * kappa
                up = s * kz
                down = s * pltpu.roll(kz, 1, 0)
                su, sv = s * u, s * v
                coef[r, p, 0] = mask - 4.0 * kk - up - down
                coef[r, p, 1] = kk - su * (8.0 / 12.0)
                coef[r, p, 2] = kk + su * (8.0 / 12.0)
                coef[r, p, 3] = su * (1.0 / 12.0)
                coef[r, p, 4] = kk - sv * (8.0 / 12.0)
                coef[r, p, 5] = kk + sv * (8.0 / 12.0)
                coef[r, p, 6] = sv * (1.0 / 12.0)
                coef[r, p, 7] = up
                coef[r, p, 8] = down
                coef[r, p, 9] = s
            return carry

        lax.fori_loop(0, count, body, 0)

    def advance(src, src_off, dst, dst_off, start, stride, count):
        def body(k, carry):
            first = start + stride * k
            for p in range(pairs):
                react = []
                for m in range(local_m):
                    part = [
                        jnp.tanh(src[m * tracers : (m + 1) * tracers, first + src_off + j, p]).reshape(wide, LANE)
                        for j in range(2)
                    ]
                    part = jnp.concatenate(part, axis=1)
                    high = part.astype(jnp.bfloat16)
                    low = (part - high.astype(jnp.float32)).astype(jnp.bfloat16)
                    both = jnp.concatenate([high, low], axis=0)
                    react.append(
                        jnp.dot(wmain[m], both, preferred_element_type=jnp.float32)
                        + jnp.dot(wlow[m], high, preferred_element_type=jnp.float32)
                    )
                for j in range(2):
                    r = first + j
                    q = r + src_off
                    k0, ke, kw, kx, ks, kn, ky, ku, kd, s = (coef[r + 2, p, i] for i in range(10))
                    for m in range(local_m):
                        mine = react[m][:, j * LANE : (j + 1) * LANE].reshape(tracers, SUB, LANE)
                        for t in range(0, tracers, CHUNK):
                            g = slice(m * tracers + t, m * tracers + t + CHUNK)
                            c = src[g, q, p]
                            swap = pltpu.roll(c, 4, 1)
                            east = pltpu.roll(src[g, q, p + 1], 4, 1) if p + 1 < pairs else 0.0
                            west = pltpu.roll(src[g, q, p - 1], 4, 1) if p > 0 else 0.0
                            xe = jnp.where(left, swap, east)
                            xw = jnp.where(left, west, swap)
                            e1 = pltpu.roll(jnp.where(lane < 1, xe, c), LANE - 1, 2)
                            e2 = pltpu.roll(jnp.where(lane < 2, xe, c), LANE - 2, 2)
                            w1 = pltpu.roll(jnp.where(lane >= LANE - 1, xw, c), 1, 2)
                            w2 = pltpu.roll(jnp.where(lane >= LANE - 2, xw, c), 2, 2)
                            total = k0 * c + s * (mine[t : t + CHUNK] - dec[g] * c)
                            total += ke * e1 + kw * w1 + kx * (e2 - w2)
                            total += ks * src[g, q + 1, p] + kn * src[g, q - 1, p]
                            total += ky * (src[g, q + 2, p] - src[g, q - 2, p])
                            total += ku * pltpu.roll(c, SUB - 1, 1) + kd * pltpu.roll(c, 1, 1)
                            dst[g, r + dst_off, p] = total
            return carry

        lax.fori_loop(0, count, body, 0)

    load_hy.wait()
    for d in range(1, members):
        hy_copy(d, lax.rem(member + members - d, members)).wait_recv()
    coefficients(0, 1, rows)
    load_tr.wait()
    advance(c0, 4, c1, 2, 2, 2, (rows - 4) // 2)

    @pl.when(has_dn)
    def _():
        tr_copy(0).wait_recv()

    @pl.when(has_up)
    def _():
        tr_copy(1).wait_recv()

    advance(c0, 4, c1, 2, 0, rows - 2, 2)
    advance(c1, 2, out, 0, 2, 2, (rows - 4) // 2)

    @pl.when(has_dn)
    def _():
        for d in range(members):
            up_copy(d, lax.rem(member + members - d, members)).wait_recv()
        wet_copy(0).wait_recv()
        tr_copy(2).wait_recv()

    @pl.when(has_up)
    def _():
        for d in range(members):
            dn_copy(d, lax.rem(member + members - d, members)).wait_recv()
        wet_copy(1).wait_recv()
        tr_copy(3).wait_recv()

    coefficients(-2, 1, 2)
    coefficients(rows, 1, 2)
    advance(c0, 4, c1, 2, -2, rows + 2, 2)
    advance(c1, 2, out, 0, 0, rows - 2, 2)

    for d in range(1, members):
        hy_copy(d, member).wait_send()

    @pl.when(has_up)
    def _():
        for d in range(members):
            up_copy(d, member).wait_send()
        for k in (0, 2):
            tr_copy(k).wait_send()
        wet_copy(0).wait_send()

    @pl.when(has_dn)
    def _():
        for d in range(members):
            dn_copy(d, member).wait_send()
        for k in (1, 3):
            tr_copy(k).wait_send()
        wet_copy(1).wait_send()


def on_device(members, tiles, tracers, hydro, wet, rates, decays):
    local_m, count, layers, rows, cols = tracers.shape
    tiles_c = cols // LANE
    pairs = tiles_c // 2
    groups = local_m * count
    conc = tracers.transpose(0, 1, 3, 2, 4).reshape(local_m, count, rows, layers, tiles_c, LANE)
    conc = conc.transpose(0, 1, 2, 4, 3, 5).reshape(groups, rows, pairs, SUB, LANE)
    planes = hydro.transpose(1, 0, 2)
    dma = pltpu.SemaphoreType.DMA
    wide = count * SUB
    vmem = pl.BlockSpec(memory_space=pltpu.VMEM)
    anywhere = pl.BlockSpec(memory_space=pl.ANY)
    result = pl.pallas_call(
        functools.partial(kernel, members, tiles),
        out_shape=jax.ShapeDtypeStruct(conc.shape, jnp.float32),
        in_specs=[anywhere, anywhere, vmem, vmem, vmem],
        out_specs=vmem,
        scratch_shapes=[
            pltpu.VMEM((groups, rows + 8, pairs, SUB, LANE), jnp.float32),
            pltpu.VMEM((groups, rows + 4, pairs, SUB, LANE), jnp.float32),
            pltpu.VMEM((members, rows + 4, planes.shape[1], LANE), jnp.float32),
            pltpu.VMEM((rows + 4, pairs, SUB, LANE), jnp.float32),
            pltpu.VMEM((rows + 4, pairs, 10, SUB, LANE), jnp.float32),
            pltpu.VMEM((local_m, wide, 2 * wide), jnp.bfloat16),
            pltpu.VMEM((local_m, wide, wide), jnp.bfloat16),
            pltpu.VMEM((groups, SUB, LANE), jnp.float32),
            dma((2,)),
            dma((4,)), dma((4,)),
            dma((max(members - 1, 1),)), dma((max(members - 1, 1),)),
            dma((members,)), dma((members,)),
            dma((members,)), dma((members,)),
            dma((2,)), dma((2,)),
        ],
        compiler_params=pltpu.CompilerParams(
            collective_id=0, has_side_effects=True, vmem_limit_bytes=48 * 1024 * 1024
        ),
    )(conc, planes, wet, rates, decays)
    result = result.reshape(local_m, count, rows, tiles_c, layers, LANE).transpose(0, 1, 2, 4, 3, 5)
    return result.reshape(local_m, count, rows, layers, cols).transpose(0, 1, 3, 2, 4)


def solution(mesh):
    placed = (
        P("member", None, None, "tile", None),
        P(None, "tile", "member"),
        P("tile", None),
        P("member", None, None),
        P("member", None),
    )
    return jax.shard_map(
        functools.partial(on_device, mesh.shape["member"], mesh.shape["tile"]),
        mesh=mesh,
        in_specs=placed,
        out_specs=P("member", None, None, "tile", None),
        check_vma=False,
    )
```

```python
import functools

import jax
import jax.numpy as jnp
from jax import lax
from jax.experimental import pallas as pl
from jax.experimental.pallas import tpu as pltpu
from jax.sharding import PartitionSpec as P

SUB, LANE = 8, 128
CHUNK = 4


def kernel(
    members, tiles, tr, hyin, wet_in, rates_in, decays_in, out,
    c0, c1, hy, wet, rates, decays, stage, hx, msk, coef, wmain, wlow, dec,
    load_sem, slow_send, slow_recv, fast_send, fast_recv, hy_send, hy_recv,
    stage_send, stage_recv, relay_send, relay_recv,
):
    tracers, local_m = rates.shape[0], rates.shape[1]
    rows, pairs = tr.shape[1], tr.shape[2]
    wide = tracers * SUB
    tile = lax.axis_index("tile")
    member = lax.axis_index("member")
    odd = lax.rem(tile, 2)
    slow_tile = tile - 1 + 2 * odd
    fast_tile = tile + 1 - 2 * odd
    has_slow = jnp.logical_and(slow_tile >= 0, slow_tile < tiles)
    slow_id = {"tile": slow_tile, "member": member}
    fast_id = {"tile": fast_tile, "member": member}

    barrier = pltpu.get_barrier_semaphore()

    def greet(where):
        pl.semaphore_signal(barrier, inc=1, device_id=where, device_id_type=pl.DeviceIdType.MESH)

    def other(d):
        return lax.rem(member + d, members)

    @pl.when(has_slow)
    def _():
        greet(slow_id)

    greet(fast_id)
    for d in range(1, members):
        greet({"tile": tile, "member": other(d)})

    loads = [
        pltpu.make_async_copy(hyin, hy.at[member], load_sem.at[0]),
        pltpu.make_async_copy(wet_in, wet, load_sem.at[1]),
        pltpu.make_async_copy(rates_in, rates, load_sem.at[2]),
        pltpu.make_async_copy(decays_in, decays, load_sem.at[3]),
        pltpu.make_async_copy(tr, c0.at[:, pl.ds(4, rows)], load_sem.at[4]),
    ]
    for load in loads:
        load.start()

    sub = lax.broadcasted_iota(jnp.int32, (SUB, LANE), 0)
    lane = lax.broadcasted_iota(jnp.int32, (SUB, LANE), 1)
    left = sub < 4

    def remote(src, dst, send, recv, where):
        return pltpu.make_async_remote_copy(
            src_ref=src, dst_ref=dst, send_sem=send, recv_sem=recv,
            device_id=where, device_id_type=pl.DeviceIdType.MESH,
        )

    def group(ref, m, row):
        return ref.at[pl.ds(m * tracers, tracers), pl.ds(row, 2)]

    def slow_copy(m, far):
        source = 2 + odd * (rows - 6) if far else odd * (rows - 2)
        target = (1 - odd) * (rows + 6) if far else rows + 4 - odd * (rows + 2)
        k = 2 * m + far
        return remote(group(tr, m, source), group(c0, m, target), slow_send.at[k], slow_recv.at[k], slow_id)

    def slow_arrival(m, far):
        target = odd * (rows + 6) if far else 2 + odd * (rows + 2)
        k = 2 * m + far
        return remote(group(tr, m, 0), group(c0, m, target), slow_send.at[k], slow_recv.at[k], slow_id)

    def fast_copy(m, far):
        source = rows - 4 - odd * (rows - 6) if far else (1 - odd) * (rows - 2)
        target = odd * (rows + 6) if far else 2 + odd * (rows + 2)
        k = 2 * m + far
        return remote(group(tr, m, source), group(c0, m, target), fast_send.at[k], fast_recv.at[k], fast_id)

    def fast_arrival(m, far):
        target = (1 - odd) * (rows + 6) if far else rows + 4 - odd * (rows + 2)
        k = 2 * m + far
        return remote(group(tr, m, 0), group(c0, m, target), fast_send.at[k], fast_recv.at[k], fast_id)

    def hy_copy(d, slot):
        return remote(
            hyin, hy.at[slot], hy_send.at[d - 1], hy_recv.at[d - 1], {"tile": tile, "member": other(d)}
        )

    def stage_copy(side):
        return remote(
            stage.at[side], hx.at[side, member], stage_send.at[side], stage_recv.at[side],
            (slow_id, fast_id)[side],
        )

    def relay_copy(side, d, slot):
        k = side * max(members - 1, 1) + d - 1
        return remote(
            hx.at[side, slot], hx.at[side, slot], relay_send.at[k], relay_recv.at[k],
            {"tile": tile, "member": other(d)},
        )

    pl.semaphore_wait(barrier, members + has_slow.astype(jnp.int32))

    @pl.when(has_slow)
    def _():
        for m in range(local_m):
            for far in range(2):
                slow_copy(m, far).start()

    for d in range(1, members):
        hy_copy(d, member).start()
    for m in range(local_m):
        for far in range(2):
            fast_copy(m, far).start()

    loads[0].wait()
    loads[1].wait()

    def wet_row(r):
        row = wet[r : r + 1, 0:LANE]
        for q in range(1, members):
            row = jnp.where(member == q, wet[r : r + 1, q * LANE : (q + 1) * LANE], row)
        return row.astype(jnp.float32)

    for j in range(2):
        low_row, high_row = wet_row(j), wet_row(rows - 2 + j)
        for side in range(2):
            low_side = odd == side
            first = odd * (rows - 2) if side == 0 else (1 - odd) * (rows - 2)
            stage[side, j, 0:15] = hy[member, first + j]
            stage[side, j, 15:16] = jnp.where(low_side, low_row, high_row)

    @pl.when(has_slow)
    def _():
        stage_copy(0).start()

    stage_copy(1).start()

    @pl.when(jnp.logical_not(has_slow))
    def _():
        c0[:, pl.ds(odd * (rows + 4), 4)] = jnp.zeros((c0.shape[0], 4) + c0.shape[2:], jnp.float32)
        hx[0] = jnp.zeros(hx.shape[1:], jnp.float32)

    loads[2].wait()
    loads[3].wait()

    for m in range(local_m):
        spread = jnp.broadcast_to(rates[:, m][:, None, :], (tracers, SUB, tracers)).reshape(wide, tracers)
        row_t = lax.broadcasted_iota(jnp.int32, (tracers, 2 * wide), 0)
        col_t = lax.broadcasted_iota(jnp.int32, (tracers, 2 * wide), 1)
        pick = (lax.rem(col_t, wide) // SUB == row_t).astype(jnp.float32)
        full = jnp.dot(spread, pick, precision=lax.Precision.HIGHEST, preferred_element_type=jnp.float32)
        row_a = lax.broadcasted_iota(jnp.int32, (wide, 2 * wide), 0)
        col_a = lax.broadcasted_iota(jnp.int32, (wide, 2 * wide), 1)
        full = jnp.where(lax.rem(row_a, SUB) == lax.rem(col_a, SUB), full, 0.0)
        high = full.astype(jnp.bfloat16)
        wmain[m] = high
        wlow[m] = (full - high.astype(jnp.float32)).astype(jnp.bfloat16)[:, :wide]
        row_d = lax.broadcasted_iota(jnp.int32, (wide, tracers), 0)
        col_d = lax.broadcasted_iota(jnp.int32, (wide, tracers), 1)
        loss = jnp.where(row_d // SUB == col_d, jnp.broadcast_to(decays[m : m + 1, :], (wide, tracers)), 0.0)
        loss = jnp.broadcast_to(jnp.sum(loss, axis=1, keepdims=True), (wide, LANE))
        dec[m * tracers : (m + 1) * tracers] = loss.reshape(tracers, SUB, LANE)

    inner_layer = lax.rem(sub, 4) != 3

    def coefficients(r, p, a0, b0, a1, b1, mask):
        u = 0.5 * jnp.where(left, a0, pltpu.roll(b0, 4, 0))
        v = 0.5 * jnp.where(left, pltpu.roll(a0, 4, 0), b0)
        kappa = 0.1 * jnp.exp(0.7 * jnp.where(left, a1, pltpu.roll(b1, 4, 0)))
        kz = 0.05 * jnp.exp(0.7 * jnp.where(left, pltpu.roll(a1, 4, 0), b1))
        kz = jnp.where(inner_layer, kz, 0.0)
        s = 0.2 * mask
        kk = s * kappa
        up = s * kz
        down = s * pltpu.roll(kz, 1, 0)
        su, sv = s * u, s * v
        coef[r, p, 0] = mask - 4.0 * kk - up - down
        coef[r, p, 1] = kk - su * (8.0 / 12.0)
        coef[r, p, 2] = kk + su * (8.0 / 12.0)
        coef[r, p, 3] = su * (1.0 / 12.0)
        coef[r, p, 4] = kk - sv * (8.0 / 12.0)
        coef[r, p, 5] = kk + sv * (8.0 / 12.0)
        coef[r, p, 6] = sv * (1.0 / 12.0)
        coef[r, p, 7] = up
        coef[r, p, 8] = down
        coef[r, p, 9] = s

    for r in range(rows):
        for p in range(pairs):
            a = jnp.broadcast_to(wet[r : r + 1, 2 * p * LANE : (2 * p + 1) * LANE], (SUB, LANE))
            b = jnp.broadcast_to(wet[r : r + 1, (2 * p + 1) * LANE : (2 * p + 2) * LANE], (SUB, LANE))
            msk[r, p] = jnp.where(left, a, b).astype(jnp.float32)

    def own_coefficients():
        def body(r, carry):
            pad = jnp.zeros((1, LANE), jnp.float32)
            for p in range(pairs):
                blocks = []
                for q in (2 * p, 2 * p + 1):
                    blocks.append(hy[q, r, 0:8])
                    blocks.append(jnp.concatenate([hy[q, r, 8:15], pad], axis=0))
                a0, a1, b0, b1 = blocks
                coefficients(r + 2, p, a0, b0, a1, b1, msk[r, p])
            return carry

        lax.fori_loop(0, rows, body, 0)

    def halo_coefficients(side):
        first = odd * (rows + 2) if side == 0 else (1 - odd) * (rows + 2)

        def body(j, carry):
            for p in range(pairs):
                a, b = 2 * p, 2 * p + 1
                mask = jnp.where(
                    left,
                    jnp.broadcast_to(hx[side, a, j, 15:16], (SUB, LANE)),
                    jnp.broadcast_to(hx[side, b, j, 15:16], (SUB, LANE)),
                )
                coefficients(
                    first + j, p, hx[side, a, j, 0:8], hx[side, b, j, 0:8],
                    hx[side, a, j, 8:16], hx[side, b, j, 8:16], mask,
                )
            return carry

        lax.fori_loop(0, 2, body, 0)

    def advance(src, src_off, dst, dst_off, start, stride, count, ms):
        def body(k, carry):
            first = start + stride * k
            for p in range(pairs):
                react = []
                for m in ms:
                    part = [
                        jnp.tanh(src[pl.ds(m * tracers, tracers), first + src_off + j, p]).reshape(wide, LANE)
                        for j in range(2)
                    ]
                    part = jnp.concatenate(part, axis=1)
                    high = part.astype(jnp.bfloat16)
                    low = (part - high.astype(jnp.float32)).astype(jnp.bfloat16)
                    both = jnp.concatenate([high, low], axis=0)
                    react.append(
                        jnp.dot(wmain[m], both, preferred_element_type=jnp.float32)
                        + jnp.dot(wlow[m], high, preferred_element_type=jnp.float32)
                    )
                for j in range(2):
                    r = first + j
                    q = r + src_off
                    k0, ke, kw, kx, ks, kn, ky, ku, kd, s = (coef[r + 2, p, i] for i in range(10))
                    for n, m in enumerate(ms):
                        mine = react[n][:, j * LANE : (j + 1) * LANE].reshape(tracers, SUB, LANE)
                        for t in range(0, tracers, CHUNK):
                            g = pl.ds(m * tracers + t, CHUNK)
                            c = src[g, q, p]
                            swap = pltpu.roll(c, 4, 1)
                            east = pltpu.roll(src[g, q, p + 1], 4, 1) if p + 1 < pairs else 0.0
                            west = pltpu.roll(src[g, q, p - 1], 4, 1) if p > 0 else 0.0
                            xe = jnp.where(left, swap, east)
                            xw = jnp.where(left, west, swap)
                            e1 = pltpu.roll(jnp.where(lane < 1, xe, c), LANE - 1, 2)
                            e2 = pltpu.roll(jnp.where(lane < 2, xe, c), LANE - 2, 2)
                            w1 = pltpu.roll(jnp.where(lane >= LANE - 1, xw, c), 1, 2)
                            w2 = pltpu.roll(jnp.where(lane >= LANE - 2, xw, c), 2, 2)
                            total = k0 * c + s * (mine[t : t + CHUNK] - dec[g] * c)
                            total += ke * e1 + kw * w1 + kx * (e2 - w2)
                            total += ks * src[g, q + 1, p] + kn * src[g, q - 1, p]
                            total += ky * (src[g, q + 2, p] - src[g, q - 2, p])
                            total += ku * pltpu.roll(c, SUB - 1, 1) + kd * pltpu.roll(c, 1, 1)
                            dst[g, r + dst_off, p] = total
            return carry

        if count == 1:
            body(0, 0)
        else:
            lax.fori_loop(0, count, body, 0)

    for d in range(1, members):
        hy_copy(d, lax.rem(member + members - d, members)).wait_recv()
    own_coefficients()
    loads[4].wait()
    every = list(range(local_m))
    advance(c0, 4, c1, 2, 2, 2, (rows - 4) // 2, every)

    def relay(side):
        stage_copy(side).wait_recv()
        for d in range(1, members):
            relay_copy(side, d, member).start()

    relay(1)

    @pl.when(has_slow)
    def _():
        relay(0)

    for m in every:
        for far in range(2):
            fast_arrival(m, far).wait_recv()
    for d in range(1, members):
        relay_copy(1, d, lax.rem(member + members - d, members)).wait_recv()
    halo_coefficients(1)
    advance(c0, 4, c1, 2, (1 - odd) * (rows - 2), 2 - 4 * odd, 2, every)
    advance(c1, 2, out, 0, 4 - 4 * odd, 2, (rows - 4) // 2, every)

    @pl.when(has_slow)
    def _():
        for d in range(1, members):
            relay_copy(0, d, lax.rem(member + members - d, members)).wait_recv()

    halo_coefficients(0)

    def last(m, carry):
        @pl.when(has_slow)
        def _():
            slow_arrival(m, 0).wait_recv()

        advance(c0, 4, c1, 2, odd * (rows - 2), 2, 1, [m])
        advance(c1, 2, out, 0, 2 + odd * (rows - 6), 2, 1, [m])

        @pl.when(has_slow)
        def _():
            slow_arrival(m, 1).wait_recv()

        advance(c0, 4, c1, 2, odd * (rows + 2) - 2, 2, 1, [m])
        advance(c1, 2, out, 0, odd * (rows - 2), 2, 1, [m])
        return carry

    lax.fori_loop(0, local_m, last, 0)

    for d in range(1, members):
        hy_copy(d, member).wait_send()
        relay_copy(1, d, member).wait_send()
    stage_copy(1).wait_send()
    for m in every:
        for far in range(2):
            fast_copy(m, far).wait_send()

    @pl.when(has_slow)
    def _():
        stage_copy(0).wait_send()
        for d in range(1, members):
            relay_copy(0, d, member).wait_send()
        for m in every:
            for far in range(2):
                slow_copy(m, far).wait_send()


def on_device(members, tiles, tracers, hydro, wet, rates, decays):
    local_m, count, layers, rows, cols = tracers.shape
    tiles_c = cols // LANE
    pairs = tiles_c // 2
    groups = local_m * count
    conc = tracers.transpose(0, 1, 3, 2, 4).reshape(local_m, count, rows, layers, tiles_c, LANE)
    conc = conc.transpose(0, 1, 2, 4, 3, 5).reshape(groups, rows, pairs, SUB, LANE)
    planes = hydro.transpose(1, 0, 2)
    coupling = rates.transpose(1, 0, 2)
    dma = pltpu.SemaphoreType.DMA
    wide = count * SUB
    depth = planes.shape[1]
    others = max(members - 1, 1)
    f32 = jnp.float32
    result = pl.pallas_call(
        functools.partial(kernel, members, tiles),
        out_shape=jax.ShapeDtypeStruct(conc.shape, f32),
        in_specs=[pl.BlockSpec(memory_space=pltpu.HBM)] * 5,
        out_specs=pl.BlockSpec(memory_space=pltpu.VMEM),
        scratch_shapes=[
            pltpu.VMEM((groups, rows + 8, pairs, SUB, LANE), f32),
            pltpu.VMEM((groups, rows + 4, pairs, SUB, LANE), f32),
            pltpu.VMEM((members, rows, depth, LANE), f32),
            pltpu.VMEM(wet.shape, wet.dtype),
            pltpu.VMEM(coupling.shape, f32),
            pltpu.VMEM(decays.shape, f32),
            pltpu.VMEM((2, 2, depth + 1, LANE), f32),
            pltpu.VMEM((2, members, 2, depth + 1, LANE), f32),
            pltpu.VMEM((rows, pairs, SUB, LANE), f32),
            pltpu.VMEM((rows + 4, pairs, 10, SUB, LANE), f32),
            pltpu.VMEM((local_m, wide, 2 * wide), jnp.bfloat16),
            pltpu.VMEM((local_m, wide, wide), jnp.bfloat16),
            pltpu.VMEM((groups, SUB, LANE), f32),
            dma((5,)),
            dma((2 * local_m,)), dma((2 * local_m,)),
            dma((2 * local_m,)), dma((2 * local_m,)),
            dma((others,)), dma((others,)),
            dma((2,)), dma((2,)),
            dma((2 * others,)), dma((2 * others,)),
        ],
        compiler_params=pltpu.CompilerParams(
            collective_id=0, has_side_effects=True, vmem_limit_bytes=48 * 1024 * 1024
        ),
    )(*(pltpu.with_memory_space_constraint(x, pltpu.HBM) for x in (conc, planes, wet, coupling, decays)))
    result = result.reshape(local_m, count, rows, tiles_c, layers, LANE).transpose(0, 1, 2, 4, 3, 5)
    return result.reshape(local_m, count, rows, layers, cols).transpose(0, 1, 3, 2, 4)


def solution(mesh):
    placed = (
        P("member", None, None, "tile", None),
        P(None, "tile", "member"),
        P("tile", None),
        P("member", None, None),
        P("member", None),
    )
    return jax.shard_map(
        functools.partial(on_device, mesh.shape["member"], mesh.shape["tile"]),
        mesh=mesh,
        in_specs=placed,
        out_specs=P("member", None, None, "tile", None),
        check_vma=False,
    )
```

```python
import functools

import jax
import jax.numpy as jnp
from jax import lax
from jax.experimental import pallas as pl
from jax.experimental.pallas import tpu as pltpu
from jax.sharding import PartitionSpec as P

SUB, LANE = 8, 128
CHUNK = 4


def kernel(
    members, tiles, tr, hyin, wet_in, rates_in, decays_in, out,
    c0, c1, hy, wet, rates, decays, stage, hx, msk, coef, wmain, wlow, dec,
    load_sem, slow_send, slow_recv, fast_send, fast_recv, hy_send, hy_recv,
    stage_send, stage_recv, relay_send, relay_recv,
):
    tracers, local_m = rates.shape[0], rates.shape[1]
    rows, pairs = tr.shape[1], tr.shape[2]
    wide = tracers * SUB
    tile = lax.axis_index("tile")
    member = lax.axis_index("member")
    odd = lax.rem(tile, 2)
    slow_tile = tile - 1 + 2 * odd
    fast_tile = tile + 1 - 2 * odd
    has_slow = jnp.logical_and(slow_tile >= 0, slow_tile < tiles)
    slow_id = {"tile": slow_tile, "member": member}
    fast_id = {"tile": fast_tile, "member": member}

    barrier = pltpu.get_barrier_semaphore()

    def greet(where):
        pl.semaphore_signal(barrier, inc=1, device_id=where, device_id_type=pl.DeviceIdType.MESH)

    def other(d):
        return lax.rem(member + d, members)

    @pl.when(has_slow)
    def _():
        greet(slow_id)

    for d in range(members):
        greet({"tile": fast_tile, "member": other(d)})
    for d in range(1, members):
        greet({"tile": tile, "member": other(d)})

    loads = [
        pltpu.make_async_copy(hyin, hy.at[member], load_sem.at[0]),
        pltpu.make_async_copy(wet_in, wet, load_sem.at[1]),
        pltpu.make_async_copy(rates_in, rates, load_sem.at[2]),
        pltpu.make_async_copy(decays_in, decays, load_sem.at[3]),
        pltpu.make_async_copy(tr, c0.at[:, pl.ds(4, rows)], load_sem.at[4]),
    ]
    for load in loads:
        load.start()

    sub = lax.broadcasted_iota(jnp.int32, (SUB, LANE), 0)
    lane = lax.broadcasted_iota(jnp.int32, (SUB, LANE), 1)
    left = sub < 4

    def remote(src, dst, send, recv, where):
        return pltpu.make_async_remote_copy(
            src_ref=src, dst_ref=dst, send_sem=send, recv_sem=recv,
            device_id=where, device_id_type=pl.DeviceIdType.MESH,
        )

    def group(ref, m, row):
        return ref.at[pl.ds(m * tracers, tracers), pl.ds(row, 2)]

    def slow_copy(m, far):
        source = 2 + odd * (rows - 6) if far else odd * (rows - 2)
        target = (1 - odd) * (rows + 6) if far else rows + 4 - odd * (rows + 2)
        k = 2 * m + far
        return remote(group(tr, m, source), group(c0, m, target), slow_send.at[k], slow_recv.at[k], slow_id)

    def slow_arrival(m, far):
        target = odd * (rows + 6) if far else 2 + odd * (rows + 2)
        k = 2 * m + far
        return remote(group(tr, m, 0), group(c0, m, target), slow_send.at[k], slow_recv.at[k], slow_id)

    def fast_copy(m, far):
        source = rows - 4 - odd * (rows - 6) if far else (1 - odd) * (rows - 2)
        target = odd * (rows + 6) if far else 2 + odd * (rows + 2)
        k = 2 * m + far
        return remote(group(tr, m, source), group(c0, m, target), fast_send.at[k], fast_recv.at[k], fast_id)

    def fast_arrival(m, far):
        target = (1 - odd) * (rows + 6) if far else rows + 4 - odd * (rows + 2)
        k = 2 * m + far
        return remote(group(tr, m, 0), group(c0, m, target), fast_send.at[k], fast_recv.at[k], fast_id)

    def hy_copy(d, slot):
        return remote(
            hyin, hy.at[slot], hy_send.at[d - 1], hy_recv.at[d - 1], {"tile": tile, "member": other(d)}
        )

    slow_stage = remote(
        stage.at[0], hx.at[0, member], stage_send.at[members], stage_recv.at[members], slow_id
    )

    def fast_stage(d, slot):
        return remote(
            stage.at[1], hx.at[1, slot], stage_send.at[d], stage_recv.at[d],
            {"tile": fast_tile, "member": other(d)},
        )

    def relay_copy(d, slot):
        return remote(
            hx.at[0, slot], hx.at[0, slot], relay_send.at[d - 1], relay_recv.at[d - 1],
            {"tile": tile, "member": other(d)},
        )

    loads[0].wait()
    loads[1].wait()

    def wet_row(r):
        row = wet[r : r + 1, 0:LANE]
        for q in range(1, members):
            row = jnp.where(member == q, wet[r : r + 1, q * LANE : (q + 1) * LANE], row)
        return row.astype(jnp.float32)

    for j in range(2):
        low_row, high_row = wet_row(j), wet_row(rows - 2 + j)
        for side in range(2):
            low_side = odd == side
            first = odd * (rows - 2) if side == 0 else (1 - odd) * (rows - 2)
            stage[side, j, 0:15] = hy[member, first + j]
            stage[side, j, 15:16] = jnp.where(low_side, low_row, high_row)

    pl.semaphore_wait(barrier, 2 * members - 1 + has_slow.astype(jnp.int32))

    @pl.when(has_slow)
    def _():
        slow_stage.start()

    for d in range(1, members):
        hy_copy(d, member).start()

    @pl.when(has_slow)
    def _():
        for m in range(local_m):
            for far in range(2):
                slow_copy(m, far).start()

    for d in range(members):
        fast_stage(d, member).start()
    for m in range(local_m):
        for far in range(2):
            fast_copy(m, far).start()

    @pl.when(jnp.logical_not(has_slow))
    def _():
        c0[:, pl.ds(odd * (rows + 4), 4)] = jnp.zeros((c0.shape[0], 4) + c0.shape[2:], jnp.float32)
        hx[0] = jnp.zeros(hx.shape[1:], jnp.float32)

    loads[2].wait()
    loads[3].wait()

    for m in range(local_m):
        spread = jnp.broadcast_to(rates[:, m][:, None, :], (tracers, SUB, tracers)).reshape(wide, tracers)
        row_t = lax.broadcasted_iota(jnp.int32, (tracers, 2 * wide), 0)
        col_t = lax.broadcasted_iota(jnp.int32, (tracers, 2 * wide), 1)
        pick = (lax.rem(col_t, wide) // SUB == row_t).astype(jnp.float32)
        full = jnp.dot(spread, pick, precision=lax.Precision.HIGHEST, preferred_element_type=jnp.float32)
        row_a = lax.broadcasted_iota(jnp.int32, (wide, 2 * wide), 0)
        col_a = lax.broadcasted_iota(jnp.int32, (wide, 2 * wide), 1)
        full = jnp.where(lax.rem(row_a, SUB) == lax.rem(col_a, SUB), full, 0.0)
        high = full.astype(jnp.bfloat16)
        wmain[m] = high
        wlow[m] = (full - high.astype(jnp.float32)).astype(jnp.bfloat16)[:, :wide]
        row_d = lax.broadcasted_iota(jnp.int32, (wide, tracers), 0)
        col_d = lax.broadcasted_iota(jnp.int32, (wide, tracers), 1)
        loss = jnp.where(row_d // SUB == col_d, jnp.broadcast_to(decays[m : m + 1, :], (wide, tracers)), 0.0)
        loss = jnp.broadcast_to(jnp.sum(loss, axis=1, keepdims=True), (wide, LANE))
        dec[m * tracers : (m + 1) * tracers] = loss.reshape(tracers, SUB, LANE)

    inner_layer = lax.rem(sub, 4) != 3

    def coefficients(r, p, a0, b0, a1, b1, mask):
        u = 0.5 * jnp.where(left, a0, pltpu.roll(b0, 4, 0))
        v = 0.5 * jnp.where(left, pltpu.roll(a0, 4, 0), b0)
        kappa = 0.1 * jnp.exp(0.7 * jnp.where(left, a1, pltpu.roll(b1, 4, 0)))
        kz = 0.05 * jnp.exp(0.7 * jnp.where(left, pltpu.roll(a1, 4, 0), b1))
        kz = jnp.where(inner_layer, kz, 0.0)
        s = 0.2 * mask
        kk = s * kappa
        up = s * kz
        down = s * pltpu.roll(kz, 1, 0)
        su, sv = s * u, s * v
        coef[r, p, 0] = mask - 4.0 * kk - up - down
        coef[r, p, 1] = kk - su * (8.0 / 12.0)
        coef[r, p, 2] = kk + su * (8.0 / 12.0)
        coef[r, p, 3] = su * (1.0 / 12.0)
        coef[r, p, 4] = kk - sv * (8.0 / 12.0)
        coef[r, p, 5] = kk + sv * (8.0 / 12.0)
        coef[r, p, 6] = sv * (1.0 / 12.0)
        coef[r, p, 7] = up
        coef[r, p, 8] = down
        coef[r, p, 9] = s

    for r in range(rows):
        for p in range(pairs):
            a = jnp.broadcast_to(wet[r : r + 1, 2 * p * LANE : (2 * p + 1) * LANE], (SUB, LANE))
            b = jnp.broadcast_to(wet[r : r + 1, (2 * p + 1) * LANE : (2 * p + 2) * LANE], (SUB, LANE))
            msk[r, p] = jnp.where(left, a, b).astype(jnp.float32)

    def own_coefficients():
        def body(r, carry):
            pad = jnp.zeros((1, LANE), jnp.float32)
            for p in range(pairs):
                blocks = []
                for q in (2 * p, 2 * p + 1):
                    blocks.append(hy[q, r, 0:8])
                    blocks.append(jnp.concatenate([hy[q, r, 8:15], pad], axis=0))
                a0, a1, b0, b1 = blocks
                coefficients(r + 2, p, a0, b0, a1, b1, msk[r, p])
            return carry

        lax.fori_loop(0, rows, body, 0)

    def halo_coefficients(side):
        first = odd * (rows + 2) if side == 0 else (1 - odd) * (rows + 2)

        def body(j, carry):
            for p in range(pairs):
                a, b = 2 * p, 2 * p + 1
                mask = jnp.where(
                    left,
                    jnp.broadcast_to(hx[side, a, j, 15:16], (SUB, LANE)),
                    jnp.broadcast_to(hx[side, b, j, 15:16], (SUB, LANE)),
                )
                coefficients(
                    first + j, p, hx[side, a, j, 0:8], hx[side, b, j, 0:8],
                    hx[side, a, j, 8:16], hx[side, b, j, 8:16], mask,
                )
            return carry

        lax.fori_loop(0, 2, body, 0)

    def advance(src, src_off, dst, dst_off, start, stride, count, ms):
        def body(k, carry):
            first = start + stride * k
            for p in range(pairs):
                react = []
                for m in ms:
                    part = [
                        jnp.tanh(src[pl.ds(m * tracers, tracers), first + src_off + j, p]).reshape(wide, LANE)
                        for j in range(2)
                    ]
                    part = jnp.concatenate(part, axis=1)
                    high = part.astype(jnp.bfloat16)
                    low = (part - high.astype(jnp.float32)).astype(jnp.bfloat16)
                    both = jnp.concatenate([high, low], axis=0)
                    react.append(
                        jnp.dot(wmain[m], both, preferred_element_type=jnp.float32)
                        + jnp.dot(wlow[m], high, preferred_element_type=jnp.float32)
                    )
                for j in range(2):
                    r = first + j
                    q = r + src_off
                    k0, ke, kw, kx, ks, kn, ky, ku, kd, s = (coef[r + 2, p, i] for i in range(10))
                    for n, m in enumerate(ms):
                        mine = react[n][:, j * LANE : (j + 1) * LANE].reshape(tracers, SUB, LANE)
                        for t in range(0, tracers, CHUNK):
                            g = pl.ds(m * tracers + t, CHUNK)
                            c = src[g, q, p]
                            swap = pltpu.roll(c, 4, 1)
                            east = pltpu.roll(src[g, q, p + 1], 4, 1) if p + 1 < pairs else 0.0
                            west = pltpu.roll(src[g, q, p - 1], 4, 1) if p > 0 else 0.0
                            xe = jnp.where(left, swap, east)
                            xw = jnp.where(left, west, swap)
                            e1 = pltpu.roll(jnp.where(lane < 1, xe, c), LANE - 1, 2)
                            e2 = pltpu.roll(jnp.where(lane < 2, xe, c), LANE - 2, 2)
                            w1 = pltpu.roll(jnp.where(lane >= LANE - 1, xw, c), 1, 2)
                            w2 = pltpu.roll(jnp.where(lane >= LANE - 2, xw, c), 2, 2)
                            total = k0 * c + s * (mine[t : t + CHUNK] - dec[g] * c)
                            total += ke * e1 + kw * w1 + kx * (e2 - w2)
                            total += ks * src[g, q + 1, p] + kn * src[g, q - 1, p]
                            total += ky * (src[g, q + 2, p] - src[g, q - 2, p])
                            total += ku * pltpu.roll(c, SUB - 1, 1) + kd * pltpu.roll(c, 1, 1)
                            dst[g, r + dst_off, p] = total
            return carry

        if count == 1:
            body(0, 0)
        else:
            lax.fori_loop(0, count, body, 0)

    for d in range(1, members):
        hy_copy(d, lax.rem(member + members - d, members)).wait_recv()
    own_coefficients()
    loads[4].wait()
    every = list(range(local_m))
    advance(c0, 4, c1, 2, 2, 2, (rows - 4) // 2, every)

    @pl.when(has_slow)
    def _():
        slow_stage.wait_recv()
        for d in range(1, members):
            relay_copy(d, member).start()

    for m in every:
        for far in range(2):
            fast_arrival(m, far).wait_recv()
    for d in range(members):
        fast_stage(d, lax.rem(member + members - d, members)).wait_recv()
    halo_coefficients(1)
    advance(c0, 4, c1, 2, (1 - odd) * (rows - 2), 2 - 4 * odd, 2, every)
    advance(c1, 2, out, 0, 4 - 4 * odd, 2, (rows - 4) // 2, every)

    @pl.when(has_slow)
    def _():
        for d in range(1, members):
            relay_copy(d, lax.rem(member + members - d, members)).wait_recv()

    halo_coefficients(0)

    def last(m, carry):
        @pl.when(has_slow)
        def _():
            slow_arrival(m, 0).wait_recv()

        advance(c0, 4, c1, 2, odd * (rows - 2), 2, 1, [m])
        advance(c1, 2, out, 0, 2 + odd * (rows - 6), 2, 1, [m])

        @pl.when(has_slow)
        def _():
            slow_arrival(m, 1).wait_recv()

        advance(c0, 4, c1, 2, odd * (rows + 2) - 2, 2, 1, [m])
        advance(c1, 2, out, 0, odd * (rows - 2), 2, 1, [m])
        return carry

    lax.fori_loop(0, local_m, last, 0)

    for d in range(1, members):
        hy_copy(d, member).wait_send()
    for d in range(members):
        fast_stage(d, member).wait_send()
    for m in every:
        for far in range(2):
            fast_copy(m, far).wait_send()

    @pl.when(has_slow)
    def _():
        slow_stage.wait_send()
        for d in range(1, members):
            relay_copy(d, member).wait_send()
        for m in every:
            for far in range(2):
                slow_copy(m, far).wait_send()


def on_device(members, tiles, tracers, hydro, wet, rates, decays):
    local_m, count, layers, rows, cols = tracers.shape
    tiles_c = cols // LANE
    pairs = tiles_c // 2
    groups = local_m * count
    conc = tracers.transpose(0, 1, 3, 2, 4).reshape(local_m, count, rows, layers, tiles_c, LANE)
    conc = conc.transpose(0, 1, 2, 4, 3, 5).reshape(groups, rows, pairs, SUB, LANE)
    planes = hydro.transpose(1, 0, 2)
    coupling = rates.transpose(1, 0, 2)
    dma = pltpu.SemaphoreType.DMA
    wide = count * SUB
    depth = planes.shape[1]
    others = max(members - 1, 1)
    f32 = jnp.float32
    result = pl.pallas_call(
        functools.partial(kernel, members, tiles),
        out_shape=jax.ShapeDtypeStruct(conc.shape, f32),
        in_specs=[pl.BlockSpec(memory_space=pltpu.HBM)] * 5,
        out_specs=pl.BlockSpec(memory_space=pltpu.VMEM),
        scratch_shapes=[
            pltpu.VMEM((groups, rows + 8, pairs, SUB, LANE), f32),
            pltpu.VMEM((groups, rows + 4, pairs, SUB, LANE), f32),
            pltpu.VMEM((members, rows, depth, LANE), f32),
            pltpu.VMEM(wet.shape, wet.dtype),
            pltpu.VMEM(coupling.shape, f32),
            pltpu.VMEM(decays.shape, f32),
            pltpu.VMEM((2, 2, depth + 1, LANE), f32),
            pltpu.VMEM((2, members, 2, depth + 1, LANE), f32),
            pltpu.VMEM((rows, pairs, SUB, LANE), f32),
            pltpu.VMEM((rows + 4, pairs, 10, SUB, LANE), f32),
            pltpu.VMEM((local_m, wide, 2 * wide), jnp.bfloat16),
            pltpu.VMEM((local_m, wide, wide), jnp.bfloat16),
            pltpu.VMEM((groups, SUB, LANE), f32),
            dma((5,)),
            dma((2 * local_m,)), dma((2 * local_m,)),
            dma((2 * local_m,)), dma((2 * local_m,)),
            dma((others,)), dma((others,)),
            dma((members + 1,)), dma((members + 1,)),
            dma((others,)), dma((others,)),
        ],
        compiler_params=pltpu.CompilerParams(
            collective_id=0, has_side_effects=True, vmem_limit_bytes=48 * 1024 * 1024
        ),
    )(*(pltpu.with_memory_space_constraint(x, pltpu.HBM) for x in (conc, planes, wet, coupling, decays)))
    result = result.reshape(local_m, count, rows, tiles_c, layers, LANE).transpose(0, 1, 2, 4, 3, 5)
    return result.reshape(local_m, count, rows, layers, cols).transpose(0, 1, 3, 2, 4)


def solution(mesh):
    placed = (
        P("member", None, None, "tile", None),
        P(None, "tile", "member"),
        P("tile", None),
        P("member", None, None),
        P("member", None),
    )
    return jax.shard_map(
        functools.partial(on_device, mesh.shape["member"], mesh.shape["tile"]),
        mesh=mesh,
        in_specs=placed,
        out_specs=P("member", None, None, "tile", None),
        check_vma=False,
    )
```
